128 devices in a mesh: leaf: 16 (over x, z), dom: 8 (over y, core).
Axes of the slice: x: 4, y: 4, z: 4, core: 2. Of those that a mesh axis runs over, the one named last changes fastest.
Arguments:
- adjoint: bfloat16 [8, 655360], P(None, ('leaf', 'dom')), may hold values from -6 to 6
- near_tiles: bfloat16 [81920, 128, 128], P(('leaf', 'dom')), may hold values from -0.25 to 0.25
- tile_rows: int32 [81920], P(('leaf', 'dom')), may hold values from 0 to 39
- tile_cols: int32 [81920], P(('leaf', 'dom')), may hold values from 0 to 119, as said below
- tile_count: int32 [128], P(('leaf', 'dom')), may hold values from 1 to 640, 49152 in all
- row_basis: bfloat16 [5120, 32, 128], P(('leaf', 'dom')), may hold values from -0.5 to 0.5
- column_basis: bfloat16 [5120, 32, 128], P(('leaf', 'dom')), may hold values from -1 to 1
- leaf_lift: float32 [5120, 32, 32], P(('leaf', 'dom')), may hold values from -0.15625 to 0.15625
- leaf_spread: float32 [5120, 32, 32], P(('leaf', 'dom')), may hold values from -1 to 1
- tree_lift: float32 [254, 32, 32], replicated, may hold values from -0.75 to 0.75
- tree_spread: float32 [254, 32, 32], replicated, may hold values from -0.75 to 0.75
- coupling: float32 [254, 4, 32, 32], replicated, may hold values from -0.625 to 0.625
- admissible: int32 [254, 4], replicated, may hold values 0 or 1
Outputs:
- applied: float32 [8, 655360], P(None, ('leaf', 'dom'))
The draws below stay inside these ranges and needn't reach their ends.
Inputs may be any that keep to these rules, and one draw needn't show every extreme that they name: Device g uses its first tile_count[g] of 640 slots; in every draw some device uses all of them. `tile_cols`: A slot's column leaf lies at most 40 leaves from its row leaf.
All inputs are finite; a program needn't handle non-finite values.
Results may differ from the reference program's by a relative error of at most 0.0003.
Values sent between devices are 32-bit elements; how exact they have to be, the bound alone decides.
No kernel may reach another device: no remote copies, remote signals or barrier semaphores. Data moves between devices by JAX's collectives and lax.ppermute only.
A program may use at most 128 MiB of HBM per device.

```python
import math
import jax
import jax.numpy as jnp
import numpy as np
from jax import lax

LEAF = 128
RANK = 32
VECS = 8
LEAVES_DEV = 40
TILES_DEV = 640
ALL_TILES = 81920
LEAVES = 5120
ELEMENTS = 655360
NODES_ALL = 254
N_LEAF = 16
N_DOM = 8


def near_pairs(key):
    rows = jax.random.randint(jax.random.fold_in(key, 11), (ALL_TILES,), 0, LEAVES_DEV)
    offsets = jax.random.randint(jax.random.fold_in(key, 12), (ALL_TILES,), -LEAVES_DEV, LEAVES_DEV + 1)
    columns = jnp.clip(LEAVES_DEV + rows + offsets, 0, 3 * LEAVES_DEV - 1)
    return (rows.astype(jnp.int32), columns.astype(jnp.int32))


def draw_tile_rows(key, part):
    rows, columns = near_pairs(key)
    return rows


def draw_tile_cols(key, part):
    rows, columns = near_pairs(key)
    return columns


def touch_ends(entries, stream_key, least, high):
    longest = entries.shape.index(max(entries.shape))
    spots = []
    for shift in (0, 1):
        where = [jax.random.randint(jax.random.fold_in(stream_key, axis), (), 0, length) for axis, length in enumerate(entries.shape)]
        where[longest] = (where[longest] + shift) % entries.shape[longest]
        spots.append(tuple(where))
    return entries.at[spots[0]].set(least).at[spots[1]].set(high)


def block_levels(rng, dims, split, smallest, top_value):
    loudness = 1.0
    for axis_at, blocks in split:
        steps = jax.random.uniform(jax.random.fold_in(jax.random.fold_in(rng, 6), axis_at), (blocks,), jnp.float32, smallest / len(split), top_value / len(split))
        loudness = loudness * jnp.repeat(jnp.exp(steps), dims[axis_at] // blocks).reshape((-1,) + (1,) * (len(dims) - 1 - axis_at))
    return loudness


def split_up(number_of, total, bound, slope):
    weights = [(1 << 20) // math.isqrt(rank ** slope) + 1 for rank in range(2, number_of + 1)]
    surplus, given = total - bound - (number_of - 1), [1] * (number_of - 1)
    while surplus > 0:
        free = [i for i in range(number_of - 1) if given[i] < bound]
        whole, left = sum([weights[i] for i in free]), surplus
        for i in free:
            more = min(bound - given[i], max(1, left * weights[i] // whole), surplus)
            given[i] = given[i] + more
            surplus = surplus - more
    return np.array([bound] + given)


def uneven(own_key, amount, total, bound, skew):
    if amount == 2:
        one = jax.random.randint(own_key, (), max(1, total - bound), min(bound, total - 1) + 1)
        return jnp.stack([one, total - one])
    tallies = jnp.asarray(split_up(amount, total, bound, skew), jnp.int32)
    twos = (amount - 1) // 2
    donor, receiver = tallies[1:1 + 2 * twos:2], tallies[2:2 + 2 * twos:2]
    slack = jnp.minimum(donor - 1, bound - receiver)
    moved = jax.random.randint(jax.random.fold_in(own_key, 1), (twos,), 0, 1 << 20) % (slack + 1)
    tallies = tallies.at[1:1 + 2 * twos:2].set(donor - moved).at[2:2 + 2 * twos:2].set(receiver + moved)
    return tallies[jax.random.permutation(jax.random.fold_in(own_key, 2), amount)]


def normal_values(rng, extent, scale, most, pieces=(), held_as=jnp.bfloat16):
    loudness = block_levels(rng, extent, pieces, -0.22, 0.18) if pieces else 1.0
    entries = jax.random.normal(rng, extent, jnp.float32) * scale * loudness
    return jnp.minimum(jnp.maximum(entries, -most), most).astype(held_as)


def setup_inputs(seed: int = 0) -> dict:
    arg_keys = jax.random.split(jax.random.key(seed), 14)
    return {
        "adjoint": normal_values(arg_keys[0], (VECS, ELEMENTS), 1.0, 6.0, ((1, 128),)),
        "near_tiles": normal_values(arg_keys[1], (ALL_TILES, LEAF, LEAF), (4 * LEAF) ** -0.5, 0.25, ((0, 128),)),
        "tile_rows": draw_tile_rows(jax.random.fold_in(arg_keys[13], 71), 0),
        "tile_cols": draw_tile_cols(jax.random.fold_in(arg_keys[13], 71), 0),
        "tile_count": uneven(arg_keys[4], N_LEAF * N_DOM, 3 * ALL_TILES // 5, TILES_DEV, 2).astype(jnp.int32),
        "row_basis": normal_values(arg_keys[5], (LEAVES, RANK, LEAF), LEAF ** -0.5, 0.5, ((0, 128),)),
        "column_basis": normal_values(arg_keys[6], (LEAVES, RANK, LEAF), RANK ** -0.5, 1.0, ((0, 128),)),
        "leaf_lift": normal_values(arg_keys[7], (LEAVES, RANK, RANK), (RANK * LEAVES_DEV) ** -0.5, 0.15625, ((0, 128),), jnp.float32),
        "leaf_spread": normal_values(arg_keys[8], (LEAVES, RANK, RANK), RANK ** -0.5, 1.0, ((0, 128),), jnp.float32),
        "tree_lift": normal_values(arg_keys[9], (NODES_ALL, RANK, RANK), (2 * RANK) ** -0.5, 0.75, (), jnp.float32),
        "tree_spread": normal_values(arg_keys[10], (NODES_ALL, RANK, RANK), (2 * RANK) ** -0.5, 0.75, (), jnp.float32),
        "coupling": normal_values(arg_keys[11], (NODES_ALL, 4, RANK, RANK), (3 * RANK) ** -0.5, 0.625, (), jnp.float32),
        "admissible": touch_ends((jax.random.randint(arg_keys[12], (NODES_ALL, 4), 0, 4) < 3).astype(jnp.int32), jax.random.fold_in(arg_keys[12], 1), 0, 1),
    }


HIGHEST = lax.Precision.HIGHEST
partner_offsets = (-3, -2, 2, 3)


def node_base(height, devices_total):
    return 2 * devices_total - 2 * (devices_total >> height)


def coarse_tree(device_nodes, tree_lift, tree_spread, coupling, admissible):
    devices_total = device_nodes.shape[0]
    heights = devices_total.bit_length() - 1
    upward = [device_nodes]
    for height in range(heights - 2):
        begin = node_base(height, devices_total)
        node_count = devices_total >> height
        lifted = jnp.einsum("nrk,nkj->nrj", upward[-1], tree_lift[begin:begin + node_count], precision=HIGHEST)
        paired = lifted.reshape((node_count // 2, 2) + lifted.shape[1:])
        upward.append(paired[:, 0] + paired[:, 1])
    coupled = []
    for height in range(heights - 1):
        begin = node_base(height, devices_total)
        node_count = devices_total >> height
        current = upward[height]
        summed = jnp.zeros_like(current)
        for slot_index, offset in enumerate(partner_offsets):
            target = jnp.arange(node_count) + offset
            inside = (target >= 0) & (target < node_count)
            partner = jnp.where(inside[:, None, None], current[jnp.clip(target, 0, node_count - 1)], 0.0)
            allowed = admissible[begin:begin + node_count, slot_index].astype(jnp.float32)
            product = jnp.einsum("nrk,nkj->nrj", partner, coupling[begin:begin + node_count, slot_index], precision=HIGHEST)
            summed = summed + allowed[:, None, None] * product
        coupled.append(summed)
    descent = coupled[heights - 2]
    for height in range(heights - 2, 0, -1):
        begin = node_base(height - 1, devices_total)
        node_count = devices_total >> (height - 1)
        spread = jnp.repeat(descent, 2, axis=0)
        descent = coupled[height - 1] + jnp.einsum("nrk,nkj->nrj", spread, tree_spread[begin:begin + node_count], precision=HIGHEST)
    return descent


def reference(adjoint, near_tiles, tile_rows, tile_cols, tile_count, row_basis, column_basis, leaf_lift, leaf_spread, tree_lift, tree_spread, coupling, admissible):
    devices_total = N_LEAF * N_DOM
    vectors = adjoint.shape[0]
    blocks = adjoint.reshape(vectors, LEAVES, LEAF).transpose(1, 0, 2)
    tiles_dev = near_tiles.reshape(devices_total, TILES_DEV, LEAF, LEAF)
    rows_dev = tile_rows.reshape(devices_total, TILES_DEV)
    cols_dev = tile_cols.reshape(devices_total, TILES_DEV)

    def add_device(running, inputs):
        position, tiles_here, rows_here, cols_here, used = inputs
        source = position * LEAVES_DEV + rows_here
        picked = blocks[source].astype(jnp.float32)
        products = jnp.einsum("trl,tlm->trm", picked, tiles_here.astype(jnp.float32), precision=HIGHEST)
        target = (position - 1) * LEAVES_DEV + cols_here
        valid = (jnp.arange(TILES_DEV) < used) & (target >= 0) & (target < LEAVES)
        weight = valid.astype(jnp.float32)
        running = running.at[jnp.where(valid, target, 0)].add(products * weight[:, None, None])
        return running, None

    start = jnp.zeros((LEAVES, vectors, LEAF), jnp.float32)
    near_field, _ = lax.scan(add_device, start, (jnp.arange(devices_total), tiles_dev, rows_dev, cols_dev, tile_count))
    upper = jnp.einsum("nrm,nkm->nrk", blocks.astype(jnp.float32), row_basis.astype(jnp.float32), precision=HIGHEST)
    grouped = upper.reshape(devices_total, LEAVES_DEV, vectors, RANK)
    lifts = leaf_lift.reshape(devices_total, LEAVES_DEV, RANK, RANK)
    device_nodes = jnp.einsum("dlrk,dlkj->drj", grouped, lifts, precision=HIGHEST)
    descent = coarse_tree(device_nodes, tree_lift, tree_spread, coupling, admissible)
    spreads = leaf_spread.reshape(devices_total, LEAVES_DEV, RANK, RANK)
    leaf_values = jnp.einsum("drk,dlkj->dlrj", descent, spreads, precision=HIGHEST).reshape(LEAVES, vectors, RANK)
    far_field = jnp.einsum("nrj,njm->nrm", leaf_values, column_basis.astype(jnp.float32), precision=HIGHEST)
    applied = near_field + far_field
    return applied.transpose(1, 0, 2).reshape(vectors, ELEMENTS)
```

```python
import functools

import jax
import jax.numpy as jnp
from jax import lax
from jax.experimental import pallas as pl
from jax.experimental.pallas import tpu as pltpu
from jax.sharding import PartitionSpec as P

AXES = ("leaf", "dom")
OFFSETS = (-3, -2, 2, 3)
DEVICES = 128
LEAVES = 40
TILES = 640
RANK = 32
VECS = 8
CHUNK = 64
CHUNKS = TILES // CHUNK
SLOTS = 4
GROUP_BASES = (0, 16, 32)

VMEM = pl.BlockSpec(memory_space=pltpu.VMEM)
SMEM = pl.BlockSpec(memory_space=pltpu.SMEM)
HBM = pl.BlockSpec(memory_space=pltpu.HBM)


def lanes(shape):
    return lax.broadcasted_iota(jnp.int32, shape, 1)


def sublanes(shape):
    return lax.broadcasted_iota(jnp.int32, shape, 0)


def split(value):
    high = value.astype(jnp.bfloat16)
    low = (value - high.astype(jnp.float32)).astype(jnp.bfloat16)
    return high, low


def fill_expanded(matrices_ref, wide_ref):
    flat = matrices_ref[...].reshape(RANK * RANK, LEAVES)
    high, low = split(flat)
    for group, base in enumerate(GROUP_BASES):
        pick = (sublanes((LEAVES, 128)) == base + lanes((LEAVES, 128)) // VECS).astype(jnp.bfloat16)
        wide = jnp.dot(high, pick, preferred_element_type=jnp.float32)
        wide = wide + jnp.dot(low, pick, preferred_element_type=jnp.float32)
        wide_ref[group] = wide.reshape(RANK, RANK, 128)


def copies(pairs, sems):
    started = [pltpu.make_async_copy(source, target, sems.at[i]) for i, (source, target) in enumerate(pairs)]
    for one in started:
        one.start()
    return started


def gather_leaves(adjoint_ref, basis_ref, lift_ref, wide_ref, coef_ref, staged):
    fill_expanded(lift_ref, wide_ref)
    lane = lanes((RANK, 128)) // VECS
    total = jnp.zeros((RANK, 128), jnp.float32)
    for group, base in enumerate(GROUP_BASES):
        count = min(16, LEAVES - base)
        stacked = [
            adjoint_ref[:, (base + c) * 128 : (base + c + 1) * 128].astype(jnp.float32) for c in range(count)
        ]
        stacked += [jnp.zeros((VECS, 128), jnp.float32)] * (16 - count)
        vectors = jnp.concatenate(stacked, axis=0).astype(jnp.bfloat16)
        basis = basis_ref[base : base + count].reshape(count * RANK, 128)
        product = lax.dot_general(
            basis, vectors, (((1,), (1,)), ((), ())), preferred_element_type=jnp.float32
        )
        coefs = jnp.zeros((RANK, 128), jnp.float32)
        for c in range(count):
            coefs = jnp.where(lane == c, product[c * RANK : (c + 1) * RANK], coefs)
        coef_ref[...] = coefs
        for k in range(RANK):
            total = total + coef_ref[k : k + 1, :] * wide_ref[group, k]
    for shift in (8, 16, 32, 64):
        total = total + pltpu.roll(total, shift, 1)
    diagonal = lanes((16, 128)) // VECS == sublanes((16, 128))
    first = jnp.sum(jnp.where(diagonal, total[:16], 0.0), axis=0, keepdims=True)
    second = jnp.sum(jnp.where(diagonal, total[16:], 0.0), axis=0, keepdims=True)
    even = sublanes((2 * DEVICES, 128)) % 2 == 0
    staged[...] = jnp.where(even, first, second)


def contract(left, right):
    dims = (((1,), (1,)), ((), ()))
    high, low = split(left)
    other, rest = split(right)
    count = left.shape[0]
    both = lax.dot_general(jnp.concatenate([high, low], axis=0), other, dims, preferred_element_type=jnp.float32)
    last = lax.dot_general(high, rest, dims, preferred_element_type=jnp.float32)
    return both[:count] + both[count:] + last


def gather_lanes(value, index):
    return jnp.take_along_axis(value, index, axis=1)


def own_position():
    return lax.axis_index("leaf") * lax.axis_size("dom") + lax.axis_index("dom")


def widen_kernel(leaf_spread_ref, wide_out):
    fill_expanded(leaf_spread_ref, wide_out)


def prepare_kernel(
    adjoint_ref,
    basis_ref,
    leaf_lift_ref,
    spread_ref,
    coupling_ref,
    admissible_ref,
    after_ref,
    payload_out,
    weight_out,
    wide_ref,
    coef_ref,
    staged,
    pieces,
    sem,
):
    gather_leaves(adjoint_ref, basis_ref, leaf_lift_ref, wide_ref, coef_ref, staged)
    write = pltpu.make_async_copy(staged, payload_out, sem)
    write.start()
    position = own_position()
    row, column = sublanes((8, 254)), lanes((8, 254))
    base = 256 - lax.shift_right_logical(jnp.full((8, 254), 256, jnp.int32), row)
    mine = base + lax.shift_right_logical(jnp.full((8, 254), position, jnp.int32), row)
    pick = ((column == mine) & (row < 6)).astype(jnp.bfloat16)
    dims = (((1,), (1,)), ((), ()))

    def extract(values, first):
        high, low = split(values.reshape(RANK * RANK, 254))
        rows = lax.dot_general(pick, high, dims, preferred_element_type=jnp.float32)
        rows = rows + lax.dot_general(pick, low, dims, preferred_element_type=jnp.float32)
        for k in range(RANK):
            pieces[first + k] = rows[:, k * RANK : (k + 1) * RANK]

    extract(spread_ref[...], 4 * RANK)
    for slot in range(4):
        extract(coupling_ref[slot], slot * RANK)

    square = (RANK, RANK)
    path = (sublanes(square) == lanes(square)).astype(jnp.float32)
    flags = jnp.concatenate([admissible_ref[...].astype(jnp.float32), jnp.zeros((4, 254), jnp.float32)], axis=0)
    flags = lax.dot_general(pick, flags.astype(jnp.bfloat16), dims, preferred_element_type=jnp.float32)
    slot = lanes((8, 128)) // RANK
    wider = (lanes((8, 128)) // RANK == sublanes((8, 128))).astype(jnp.bfloat16)
    flags = jnp.dot(flags.astype(jnp.bfloat16), wider, preferred_element_type=jnp.float32)
    level = sublanes((8, 128))
    other = lax.shift_right_logical(jnp.full((8, 128), position, jnp.int32), level)
    other = other + jnp.where(slot < 2, slot - 3, slot)
    size = lax.shift_right_logical(jnp.full((8, 128), DEVICES, jnp.int32), level)
    flags = jnp.where((other >= 0) & (other < size), flags, 0.0)
    for height in range(6):
        if height:
            path = contract(path, pieces[4 * RANK : 5 * RANK, height - 1, :])
        allowed = flags[height : height + 1]
        high, low = split(contract(path, pieces[: 4 * RANK, height, :]) * allowed)
        weight_out[:RANK, height * 128 : (height + 1) * 128] = high
        weight_out[RANK:, height * 128 : (height + 1) * 128] = low
    write.wait()


def near_kernel(
    count_ref,
    rows_hbm,
    cols_hbm,
    adjoint_hbm,
    tiles_ref,
    own_ref,
    chip_ref,
    far_ref,
    rows_ref,
    cols_ref,
    adjoint_ref,
    buffer,
    uppers,
    lowers,
    sums,
    small_sems,
    sems,
):
    arriving = copies([(rows_hbm, rows_ref), (cols_hbm, cols_ref), (adjoint_hbm, adjoint_ref)], small_sems)
    used = count_ref[0]
    chunks = lax.div(used + (CHUNK - 1), CHUNK)

    def copy(c):
        slot = lax.rem(c, SLOTS)
        target = buffer.at[pl.ds(slot * CHUNK, CHUNK)]
        return pltpu.make_async_copy(tiles_ref.at[pl.ds(c * CHUNK, CHUNK)], target, sems.at[slot])

    def start(c, carry):
        copy(c).start()
        return carry

    lax.fori_loop(0, jnp.minimum(chunks, SLOTS), start, 0)
    sums[...] = jnp.zeros_like(sums)
    for one in arriving:
        one.wait()
    blank = jnp.zeros((VECS, 128), jnp.float32)
    for c in range(LEAVES):
        vectors = adjoint_ref[:, c * 128 : (c + 1) * 128].astype(jnp.float32)
        uppers[c] = jnp.concatenate([vectors, blank], axis=0).astype(jnp.bfloat16)
        lowers[c] = jnp.concatenate([blank, vectors], axis=0).astype(jnp.bfloat16)

    def body(c, carry):
        copy(c).wait()
        first = c * CHUNK
        held = lax.rem(c, SLOTS) * CHUNK
        products = []
        for j in range(0, CHUNK, 2):
            left = jnp.concatenate([uppers[rows_ref[first + j]], lowers[rows_ref[first + j + 1]]], axis=1)
            right = buffer[pl.ds(held + j, 2)].reshape(256, 128)
            both = jnp.dot(left, right, preferred_element_type=jnp.float32)
            products += [both[:VECS], both[VECS:]]
        for j in range(CHUNK):
            target = jnp.where(first + j < used, cols_ref[first + j], 3 * LEAVES)
            sums[target] = sums[target] + products[j]

        @pl.when(c + SLOTS < chunks)
        def _():
            copy(c + SLOTS).start()

        return carry

    lax.fori_loop(0, chunks, body, 0)
    odd = lax.rem(lax.axis_index("dom"), 2)
    own_ref[...] = sums[LEAVES : 2 * LEAVES]
    chip_ref[...] = sums[pl.ds((1 - odd) * 2 * LEAVES, LEAVES)]
    position = own_position()
    inside = (position > 0) & (position < DEVICES - 1)
    far_ref[...] = jnp.where(inside, sums[pl.ds(odd * 2 * LEAVES, LEAVES)], 0.0)


def lift_level(source, count, matrix, inner_steps=4):
    def body(step, totals):
        for inner in range(inner_steps):
            k = step * inner_steps + inner
            values = matrix(k)
            totals = tuple(totals[r] + source[k, r : r + 1, :] * values for r in range(count))
        return totals

    start = tuple(jnp.zeros((RANK, 128), jnp.float32) for _ in range(count))
    if inner_steps == RANK:
        return body(0, start)
    return lax.fori_loop(0, RANK // inner_steps, body, start)


def tree_kernel(gathered_ref, weight_ref, lift_ref, down_ref, up0, up, partners):
    position = own_position()
    lane = lanes((RANK, 128))
    vector = lane % VECS

    def put(height, slot, values):
        high, low = split(values)
        first = (height * 4 + slot) * RANK
        partners[first : first + RANK, :128] = high
        partners[first : first + RANK, 128:] = low

    def partner(height, offset):
        return jnp.clip((position >> height) + offset, 0, (DEVICES >> height) - 1)

    for half in range(2):
        block = gathered_ref[pl.ds(half, DEVICES, stride=2), :].T
        up0[half * 16 : (half + 1) * 16] = block.reshape(16, VECS, 128)
    spot = sublanes((16, 128)) * VECS + lanes((16, 128)) % VECS
    for slot, offset in enumerate(OFFSETS):
        rows = gathered_ref[pl.ds(2 * partner(0, offset), 2), :]
        halves = [gather_lanes(jnp.broadcast_to(rows[i : i + 1], (16, 128)), spot) for i in range(2)]
        put(0, slot, jnp.concatenate(halves, axis=0))

    level = lift_level(up0, VECS, lambda k: lift_ref[k, :, :128])
    for height in range(1, 6):
        nodes = DEVICES >> height
        width = max(nodes, 16)
        paired = [values + pltpu.roll(values, 127, 1) for values in level]
        if height <= 3:
            index = lane // (2 * width) * (2 * width) + 2 * (lane % width)
            if height == 1:
                index = 2 * (lane % 64)
            count = len(paired) // 2
            second = (lane // width) % 2 == 1
            level = [
                jnp.where(second, gather_lanes(paired[r + count], index), gather_lanes(paired[r], index))
                for r in range(count)
            ]
        else:
            count = 1
            level = [gather_lanes(paired[0], lane // 16 * 16 + 2 * (lane % nodes))]
        for slot, offset in enumerate(OFFSETS):
            place = vector // count * width + partner(height, offset)
            chosen = gather_lanes(level[0], place)
            for r in range(1, count):
                chosen = jnp.where(vector % count == r, gather_lanes(level[r], place), chosen)
            put(height, slot, chosen)
        if height < 5:
            for r in range(count):
                up[:, r, :] = level[r]
            spot = 128 - (256 >> height) + lane % nodes

            def repeated(k, spot=spot):
                tail = jnp.concatenate([lift_ref[k, :, 128:254], jnp.zeros((RANK, 2), jnp.float32)], axis=1)
                return gather_lanes(tail, spot)

            level = lift_level(up, count, repeated, RANK)

    product = jnp.dot(weight_ref[...], partners[...], preferred_element_type=jnp.float32)
    down_ref[...] = product[:RANK, :128] + product[:RANK, 128:] + product[RANK:, :128]


def final_kernel(down, wide_ref, basis_ref, own_ref, chip_ref, far_ref, out_ref):
    square = lanes((128, 128)) // RANK == (sublanes((128, 128)) // VECS) % 4
    for group, base in enumerate(GROUP_BASES):
        count = min(16, LEAVES - base)
        total = jnp.zeros((RANK, 128), jnp.float32)
        for k in range(RANK):
            total = total + down[k : k + 1, :] * wide_ref[group, k]
        values = jnp.where(square, jnp.concatenate([total] * 4, axis=0).T, 0.0)
        for quad in range(count // 4):
            high, low = split(values[quad * 32 : (quad + 1) * 32])
            leaf = base + quad * 4
            matrix = basis_ref[leaf : leaf + 4].reshape(128, 128)
            both = jnp.dot(jnp.concatenate([high, low], axis=0), matrix, preferred_element_type=jnp.float32)
            part = slice(leaf, leaf + 4)
            near = own_ref[part] + (chip_ref[part] + far_ref[part])
            out_ref[part] = near + (both[:32] + both[32:]).reshape(4, VECS, 128)


def local(
    adjoint,
    near_tiles,
    tile_rows,
    tile_cols,
    tile_count,
    row_basis,
    column_basis,
    leaf_lift,
    leaf_spread,
    tree_lift,
    tree_spread,
    coupling,
    admissible,
):
    f32 = jnp.float32
    by_leaf = lambda x: jnp.transpose(x, (1, 2, 0))
    in_hbm = lambda x: pltpu.with_memory_space_constraint(x, pltpu.HBM)
    window = jax.ShapeDtypeStruct((LEAVES, VECS, 128), f32)
    own, chip, far = pl.pallas_call(
        near_kernel,
        out_shape=(window, window, window),
        in_specs=[SMEM] + [HBM] * 4,
        out_specs=(VMEM, VMEM, VMEM),
        scratch_shapes=[
            pltpu.SMEM((TILES,), jnp.int32),
            pltpu.SMEM((TILES,), jnp.int32),
            pltpu.VMEM((VECS, LEAVES * 128), jnp.bfloat16),
            pltpu.VMEM((SLOTS * CHUNK, 128, 128), jnp.bfloat16),
            pltpu.VMEM((LEAVES, 2 * VECS, 128), jnp.bfloat16),
            pltpu.VMEM((LEAVES, 2 * VECS, 128), jnp.bfloat16),
            pltpu.VMEM((3 * LEAVES + 8, VECS, 128), f32),
            pltpu.SemaphoreType.DMA((3,)),
            pltpu.SemaphoreType.DMA((SLOTS,)),
        ],
        compiler_params=pltpu.CompilerParams(vmem_limit_bytes=14 * 2**20),
        cost_estimate=pl.CostEstimate(flops=10_000_000_000, bytes_accessed=30_000_000, transcendentals=0),
        name="near",
    )(tile_count, in_hbm(tile_rows), in_hbm(tile_cols), in_hbm(adjoint), in_hbm(near_tiles))
    payload, weights = pl.pallas_call(
        prepare_kernel,
        out_shape=(
            pltpu.HBM((2 * DEVICES, 128), f32),
            jax.ShapeDtypeStruct((2 * RANK, 24 * RANK), jnp.bfloat16),
        ),
        in_specs=[VMEM] * 6 + [pl.BlockSpec(memory_space=pl.ANY)],
        out_specs=(HBM, VMEM),
        scratch_shapes=[
            pltpu.VMEM((3, RANK, RANK, 128), f32),
            pltpu.VMEM((RANK, 128), f32),
            pltpu.VMEM((2 * DEVICES, 128), f32),
            pltpu.VMEM((5 * RANK, 8, RANK), f32),
            pltpu.SemaphoreType.DMA,
        ],
        compiler_params=pltpu.CompilerParams(vmem_limit_bytes=8 * 2**20),
        cost_estimate=pl.CostEstimate(flops=4_000_000_000, bytes_accessed=12_000_000, transcendentals=0),
        name="prepare",
    )(
        adjoint,
        row_basis,
        by_leaf(leaf_lift),
        by_leaf(tree_spread),
        jnp.transpose(coupling, (1, 2, 3, 0)),
        admissible.T,
        own,
    )
    gathered = lax.all_to_all(payload, AXES, 0, 0, tiled=True)
    across = [(i, (i + 1) % DEVICES) for i in range(1, DEVICES, 2)]
    far = lax.ppermute(far, AXES, across + [(b, a) for a, b in across])
    within = [(i, i ^ 1) for i in range(DEVICES)]
    chip = lax.ppermute(chip, AXES, within)

    wide = pl.pallas_call(
        widen_kernel,
        out_shape=jax.ShapeDtypeStruct((3, RANK, RANK, 128), f32),
        in_specs=[VMEM],
        out_specs=VMEM,
        compiler_params=pltpu.CompilerParams(vmem_limit_bytes=4 * 2**20),
        cost_estimate=pl.CostEstimate(flops=1_000_000_000, bytes_accessed=3_000_000, transcendentals=0),
        name="widen",
    )(by_leaf(leaf_spread))
    down = pl.pallas_call(
        tree_kernel,
        out_shape=jax.ShapeDtypeStruct((RANK, 128), f32),
        in_specs=[VMEM] * 3,
        out_specs=VMEM,
        scratch_shapes=[
            pltpu.VMEM((RANK, VECS, 128), f32),
            pltpu.VMEM((RANK, VECS, 128), f32),
            pltpu.VMEM((24 * RANK, 256), jnp.bfloat16),
        ],
        compiler_params=pltpu.CompilerParams(vmem_limit_bytes=8 * 2**20),
        cost_estimate=pl.CostEstimate(flops=4_000_000_000, bytes_accessed=6_000_000, transcendentals=0),
        name="tree",
    )(gathered, weights, by_leaf(tree_lift))
    out = pl.pallas_call(
        final_kernel,
        out_shape=window,
        in_specs=[VMEM] * 6,
        out_specs=VMEM,
        compiler_params=pltpu.CompilerParams(vmem_limit_bytes=8 * 2**20),
        cost_estimate=pl.CostEstimate(flops=100_000_000, bytes_accessed=3_000_000, transcendentals=0),
        name="final",
    )(down, wide, column_basis, own, chip, far)
    return out.transpose(1, 0, 2).reshape(VECS, LEAVES * 128)


def solution(mesh):
    part = P(AXES, None, None)
    return jax.shard_map(
        local,
        mesh=mesh,
        in_specs=(P(None, AXES), part, P(AXES), P(AXES), P(AXES), part, part, part, part, P(), P(), P(), P()),
        out_specs=P(None, AXES),
        check_vma=False,
    )
```

```python
import functools

import jax
import jax.numpy as jnp
from jax import lax
from jax.experimental import pallas as pl
from jax.experimental.pallas import tpu as pltpu
from jax.sharding import PartitionSpec as P

AXES = ("leaf", "dom")
OFFSETS = (-3, -2, 2, 3)
DEVICES = 128
LEAVES = 40
TILES = 640
RANK = 32
VECS = 8
CHUNK = 64
CHUNKS = TILES // CHUNK
GROUP_BASES = (0, 16, 32)

VMEM = pl.BlockSpec(memory_space=pltpu.VMEM)
SMEM = pl.BlockSpec(memory_space=pltpu.SMEM)
HBM = pl.BlockSpec(memory_space=pltpu.HBM)


def lanes(shape):
    return lax.broadcasted_iota(jnp.int32, shape, 1)


def sublanes(shape):
    return lax.broadcasted_iota(jnp.int32, shape, 0)


def split(value):
    high = value.astype(jnp.bfloat16)
    low = (value - high.astype(jnp.float32)).astype(jnp.bfloat16)
    return high, low


def fill_expanded(matrices_ref, wide_ref):
    flat = matrices_ref[...].reshape(RANK * RANK, LEAVES)
    high, low = split(flat)
    for group, base in enumerate(GROUP_BASES):
        pick = (sublanes((LEAVES, 128)) == base + lanes((LEAVES, 128)) // VECS).astype(jnp.bfloat16)
        wide = jnp.dot(high, pick, preferred_element_type=jnp.float32)
        wide = wide + jnp.dot(low, pick, preferred_element_type=jnp.float32)
        wide_ref[group] = wide.reshape(RANK, RANK, 128)


def copies(pairs, sems):
    started = [pltpu.make_async_copy(source, target, sems.at[i]) for i, (source, target) in enumerate(pairs)]
    for one in started:
        one.start()
    return started


def gather_leaves(adjoint_ref, basis_ref, lift_ref, wide_ref, coef_ref, staged):
    fill_expanded(lift_ref, wide_ref)
    lane = lanes((RANK, 128)) // VECS
    total = jnp.zeros((RANK, 128), jnp.float32)
    for group, base in enumerate(GROUP_BASES):
        count = min(16, LEAVES - base)
        stacked = [
            adjoint_ref[:, (base + c) * 128 : (base + c + 1) * 128].astype(jnp.float32) for c in range(count)
        ]
        stacked += [jnp.zeros((VECS, 128), jnp.float32)] * (16 - count)
        vectors = jnp.concatenate(stacked, axis=0).astype(jnp.bfloat16)
        basis = basis_ref[base : base + count].reshape(count * RANK, 128)
        product = lax.dot_general(
            basis, vectors, (((1,), (1,)), ((), ())), preferred_element_type=jnp.float32
        )
        coefs = jnp.zeros((RANK, 128), jnp.float32)
        for c in range(count):
            coefs = jnp.where(lane == c, product[c * RANK : (c + 1) * RANK], coefs)
        coef_ref[...] = coefs
        for k in range(RANK):
            total = total + coef_ref[k : k + 1, :] * wide_ref[group, k]
    for shift in (8, 16, 32, 64):
        total = total + pltpu.roll(total, shift, 1)
    diagonal = lanes((16, 128)) // VECS == sublanes((16, 128))
    first = jnp.sum(jnp.where(diagonal, total[:16], 0.0), axis=0, keepdims=True)
    second = jnp.sum(jnp.where(diagonal, total[16:], 0.0), axis=0, keepdims=True)
    even = sublanes((2 * DEVICES, 128)) % 2 == 0
    staged[...] = jnp.where(even, first, second)


def contract(left, right):
    dims = (((1,), (1,)), ((), ()))
    high, low = split(left)
    other, rest = split(right)
    count = left.shape[0]
    both = lax.dot_general(jnp.concatenate([high, low], axis=0), other, dims, preferred_element_type=jnp.float32)
    last = lax.dot_general(high, rest, dims, preferred_element_type=jnp.float32)
    return both[:count] + both[count:] + last


def gather_lanes(value, index):
    return jnp.take_along_axis(value, index, axis=1)


def own_position():
    return lax.axis_index("leaf") * lax.axis_size("dom") + lax.axis_index("dom")


def works_late():
    leaf, dom = lax.axis_index("leaf"), lax.axis_index("dom")
    return 4 * (leaf // 4) + 8 * (leaf % 4) + 5 * (dom // 2) >= 30


def weigh(spread_ref, coupling_ref, admissible_ref, weight_out, pieces):
    position = own_position()
    row, column = sublanes((8, 254)), lanes((8, 254))
    base = 256 - lax.shift_right_logical(jnp.full((8, 254), 256, jnp.int32), row)
    mine = base + lax.shift_right_logical(jnp.full((8, 254), position, jnp.int32), row)
    pick = ((column == mine) & (row < 6)).astype(jnp.bfloat16)
    dims = (((1,), (1,)), ((), ()))

    def extract(values, first):
        high, low = split(values.reshape(RANK * RANK, 254))
        rows = lax.dot_general(pick, high, dims, preferred_element_type=jnp.float32)
        rows = rows + lax.dot_general(pick, low, dims, preferred_element_type=jnp.float32)
        for k in range(RANK):
            pieces[first + k] = rows[:, k * RANK : (k + 1) * RANK]

    extract(spread_ref[...], 4 * RANK)
    for slot in range(4):
        extract(coupling_ref[slot], slot * RANK)

    flags = jnp.concatenate([admissible_ref[...].astype(jnp.float32), jnp.zeros((4, 254), jnp.float32)], axis=0)
    flags = lax.dot_general(pick, flags.astype(jnp.bfloat16), dims, preferred_element_type=jnp.float32)
    slot = lanes((8, 128)) // RANK
    wider = (lanes((8, 128)) // RANK == sublanes((8, 128))).astype(jnp.bfloat16)
    flags = jnp.dot(flags.astype(jnp.bfloat16), wider, preferred_element_type=jnp.float32)
    level = sublanes((8, 128))
    other = lax.shift_right_logical(jnp.full((8, 128), position, jnp.int32), level)
    other = other + jnp.where(slot < 2, slot - 3, slot)
    size = lax.shift_right_logical(jnp.full((8, 128), DEVICES, jnp.int32), level)
    flags = jnp.where((other >= 0) & (other < size), flags, 0.0)
    square = (RANK, RANK)
    path = (sublanes(square) == lanes(square)).astype(jnp.float32)
    for height in range(6):
        if height:
            path = contract(path, pieces[4 * RANK : 5 * RANK, height - 1, :])
        allowed = flags[height : height + 1]
        high, low = split(contract(path, pieces[: 4 * RANK, height, :]) * allowed)
        weight_out[:RANK, height * 128 : (height + 1) * 128] = high
        weight_out[RANK:, height * 128 : (height + 1) * 128] = low


def widen_kernel(
    leaf_spread_hbm,
    early_ref,
    spread_hbm,
    coupling_hbm,
    admissible_hbm,
    wide_out,
    weight_out,
    weight_ref,
    leaf_spread_ref,
    spread_ref,
    coupling_ref,
    admissible_ref,
    pieces,
    sems,
):
    late = works_late()
    leaf_spreads = pltpu.make_async_copy(leaf_spread_hbm, leaf_spread_ref, sems.at[3])
    leaf_spreads.start()

    @pl.when(late)
    def _():
        copies(
            [(spread_hbm, spread_ref), (coupling_hbm, coupling_ref), (admissible_hbm, admissible_ref)], sems
        )

    leaf_spreads.wait()
    fill_expanded(leaf_spread_ref, wide_out)

    @pl.when(late)
    def _():
        pltpu.make_async_copy(spread_hbm, spread_ref, sems.at[0]).wait()
        pltpu.make_async_copy(coupling_hbm, coupling_ref, sems.at[1]).wait()
        pltpu.make_async_copy(admissible_hbm, admissible_ref, sems.at[2]).wait()
        weigh(spread_ref, coupling_ref, admissible_ref, weight_ref, pieces)

    @pl.when(jnp.logical_not(late))
    def _():
        weight_ref[...] = early_ref[...]

    write = pltpu.make_async_copy(weight_ref, weight_out, sems.at[4])
    write.start()
    write.wait()


def near_kernel(
    count_ref,
    rows_hbm,
    cols_hbm,
    adjoint_hbm,
    tiles_ref,
    basis_hbm,
    leaf_lift_hbm,
    spread_hbm,
    coupling_hbm,
    admissible_hbm,
    payload_out,
    weight_out,
    own_ref,
    chip_ref,
    far_ref,
    rows_ref,
    cols_ref,
    adjoint_ref,
    basis_ref,
    leaf_lift_ref,
    spread_ref,
    coupling_ref,
    admissible_ref,
    pieces,
    wide_ref,
    coef_ref,
    staged,
    buffer,
    uppers,
    lowers,
    sums,
    small_sems,
    table_sems,
    sems,
):
    early = jnp.logical_not(works_late())
    tables = [(spread_hbm, spread_ref), (coupling_hbm, coupling_ref), (admissible_hbm, admissible_ref)]
    arriving = copies(
        [
            (leaf_lift_hbm, leaf_lift_ref),
            (basis_hbm, basis_ref),
            (adjoint_hbm, adjoint_ref),
            (rows_hbm, rows_ref),
            (cols_hbm, cols_ref),
        ],
        small_sems,
    )

    @pl.when(early)
    def _():
        copies(tables, table_sems)

    used = count_ref[0]
    chunks = lax.div(used + (CHUNK - 1), CHUNK)

    def copy(c):
        part = pl.ds(c * CHUNK, CHUNK)
        return pltpu.make_async_copy(tiles_ref.at[part], buffer.at[part], sems.at[c])

    def start(c, carry):
        copy(c).start()
        return carry

    lax.fori_loop(0, chunks, start, 0)
    sums[...] = jnp.zeros_like(sums)
    for one in arriving:
        one.wait()
    blank = jnp.zeros((VECS, 128), jnp.float32)
    for c in range(LEAVES):
        vectors = adjoint_ref[:, c * 128 : (c + 1) * 128].astype(jnp.float32)
        uppers[c] = jnp.concatenate([vectors, blank], axis=0).astype(jnp.bfloat16)
        lowers[c] = jnp.concatenate([blank, vectors], axis=0).astype(jnp.bfloat16)
    gather_leaves(adjoint_ref, basis_ref, leaf_lift_ref, wide_ref, coef_ref, staged)
    write = pltpu.make_async_copy(staged, payload_out, small_sems.at[5])
    write.start()

    @pl.when(early)
    def _():
        for i, (source, target) in enumerate(tables):
            pltpu.make_async_copy(source, target, table_sems.at[i]).wait()
        weigh(spread_ref, coupling_ref, admissible_ref, weight_out, pieces)

    def body(c, carry):
        copy(c).wait()
        first = c * CHUNK
        products = []
        for j in range(0, CHUNK, 2):
            left = jnp.concatenate([uppers[rows_ref[first + j]], lowers[rows_ref[first + j + 1]]], axis=1)
            right = buffer[pl.ds(first + j, 2)].reshape(256, 128)
            both = jnp.dot(left, right, preferred_element_type=jnp.float32)
            products += [both[:VECS], both[VECS:]]
        for j in range(CHUNK):
            target = jnp.where(first + j < used, cols_ref[first + j], 3 * LEAVES)
            sums[target] = sums[target] + products[j]
        return carry

    lax.fori_loop(0, chunks, body, 0)
    write.wait()
    odd = lax.rem(lax.axis_index("dom"), 2)
    own_ref[...] = sums[LEAVES : 2 * LEAVES]
    chip_ref[...] = sums[pl.ds((1 - odd) * 2 * LEAVES, LEAVES)]
    position = own_position()
    inside = (position > 0) & (position < DEVICES - 1)
    far_ref[...] = jnp.where(inside, sums[pl.ds(odd * 2 * LEAVES, LEAVES)], 0.0)


def lift_level(source, count, matrix, inner_steps=4):
    def body(step, totals):
        for inner in range(inner_steps):
            k = step * inner_steps + inner
            values = matrix(k)
            totals = tuple(totals[r] + source[k, r : r + 1, :] * values for r in range(count))
        return totals

    start = tuple(jnp.zeros((RANK, 128), jnp.float32) for _ in range(count))
    if inner_steps == RANK:
        return body(0, start)
    return lax.fori_loop(0, RANK // inner_steps, body, start)


def tree_kernel(gathered_ref, weight_hbm, lift_ref, down_ref, up0, up, partners, weight_ref, sem):
    weights = pltpu.make_async_copy(weight_hbm, weight_ref, sem)
    weights.start()
    position = own_position()
    lane = lanes((RANK, 128))
    vector = lane % VECS

    def put(height, slot, values):
        high, low = split(values)
        first = (height * 4 + slot) * RANK
        partners[first : first + RANK, :128] = high
        partners[first : first + RANK, 128:] = low

    def partner(height, offset):
        return jnp.clip((position >> height) + offset, 0, (DEVICES >> height) - 1)

    for half in range(2):
        block = gathered_ref[pl.ds(half, DEVICES, stride=2), :].T
        up0[half * 16 : (half + 1) * 16] = block.reshape(16, VECS, 128)
    spot = sublanes((16, 128)) * VECS + lanes((16, 128)) % VECS
    for slot, offset in enumerate(OFFSETS):
        rows = gathered_ref[pl.ds(2 * partner(0, offset), 2), :]
        halves = [gather_lanes(jnp.broadcast_to(rows[i : i + 1], (16, 128)), spot) for i in range(2)]
        put(0, slot, jnp.concatenate(halves, axis=0))

    level = lift_level(up0, VECS, lambda k: lift_ref[k, :, :128])
    for height in range(1, 6):
        nodes = DEVICES >> height
        width = max(nodes, 16)
        paired = [values + pltpu.roll(values, 127, 1) for values in level]
        if height <= 3:
            index = lane // (2 * width) * (2 * width) + 2 * (lane % width)
            if height == 1:
                index = 2 * (lane % 64)
            count = len(paired) // 2
            second = (lane // width) % 2 == 1
            level = [
                jnp.where(second, gather_lanes(paired[r + count], index), gather_lanes(paired[r], index))
                for r in range(count)
            ]
        else:
            count = 1
            level = [gather_lanes(paired[0], lane // 16 * 16 + 2 * (lane % nodes))]
        for slot, offset in enumerate(OFFSETS):
            place = vector // count * width + partner(height, offset)
            chosen = gather_lanes(level[0], place)
            for r in range(1, count):
                chosen = jnp.where(vector % count == r, gather_lanes(level[r], place), chosen)
            put(height, slot, chosen)
        if height < 5:
            for r in range(count):
                up[:, r, :] = level[r]
            spot = 128 - (256 >> height) + lane % nodes

            def repeated(k, spot=spot):
                tail = jnp.concatenate([lift_ref[k, :, 128:254], jnp.zeros((RANK, 2), jnp.float32)], axis=1)
                return gather_lanes(tail, spot)

            level = lift_level(up, count, repeated, RANK)

    weights.wait()
    product = jnp.dot(weight_ref[...], partners[...], preferred_element_type=jnp.float32)
    down_ref[...] = product[:RANK, :128] + product[:RANK, 128:] + product[RANK:, :128]


def final_kernel(down, wide_ref, basis_ref, own_ref, chip_ref, far_ref, out_ref):
    square = lanes((128, 128)) // RANK == (sublanes((128, 128)) // VECS) % 4
    for group, base in enumerate(GROUP_BASES):
        count = min(16, LEAVES - base)
        total = jnp.zeros((RANK, 128), jnp.float32)
        for k in range(RANK):
            total = total + down[k : k + 1, :] * wide_ref[group, k]
        values = jnp.where(square, jnp.concatenate([total] * 4, axis=0).T, 0.0)
        for quad in range(count // 4):
            high, low = split(values[quad * 32 : (quad + 1) * 32])
            leaf = base + quad * 4
            matrix = basis_ref[leaf : leaf + 4].reshape(128, 128)
            both = jnp.dot(jnp.concatenate([high, low], axis=0), matrix, preferred_element_type=jnp.float32)
            part = slice(leaf, leaf + 4)
            near = own_ref[part] + (chip_ref[part] + far_ref[part])
            out_ref[part] = near + (both[:32] + both[32:]).reshape(4, VECS, 128)


def local(
    adjoint,
    near_tiles,
    tile_rows,
    tile_cols,
    tile_count,
    row_basis,
    column_basis,
    leaf_lift,
    leaf_spread,
    tree_lift,
    tree_spread,
    coupling,
    admissible,
):
    f32 = jnp.float32
    by_leaf = lambda x: jnp.transpose(x, (1, 2, 0))
    in_hbm = lambda x: pltpu.with_memory_space_constraint(x, pltpu.HBM)
    window = jax.ShapeDtypeStruct((LEAVES, VECS, 128), f32)
    spread_table = in_hbm(by_leaf(tree_spread))
    coupling_table = in_hbm(jnp.transpose(coupling, (1, 2, 3, 0)))
    admissible_table = in_hbm(admissible.T)
    payload, weights, own, chip, far = pl.pallas_call(
        near_kernel,
        out_shape=(
            pltpu.HBM((2 * DEVICES, 128), f32),
            jax.ShapeDtypeStruct((2 * RANK, 24 * RANK), jnp.bfloat16),
            window,
            window,
            window,
        ),
        in_specs=[SMEM] + [HBM] * 9,
        out_specs=(HBM, VMEM, VMEM, VMEM, VMEM),
        scratch_shapes=[
            pltpu.SMEM((TILES,), jnp.int32),
            pltpu.SMEM((TILES,), jnp.int32),
            pltpu.VMEM((VECS, LEAVES * 128), jnp.bfloat16),
            pltpu.VMEM((LEAVES, RANK, 128), jnp.bfloat16),
            pltpu.VMEM((RANK, RANK, LEAVES), f32),
            pltpu.VMEM((RANK, RANK, 254), f32),
            pltpu.VMEM((4, RANK, RANK, 254), f32),
            pltpu.VMEM((4, 254), jnp.int32),
            pltpu.VMEM((5 * RANK, 8, RANK), f32),
            pltpu.VMEM((3, RANK, RANK, 128), f32),
            pltpu.VMEM((RANK, 128), f32),
            pltpu.VMEM((2 * DEVICES, 128), f32),
            pltpu.VMEM((TILES, 128, 128), jnp.bfloat16),
            pltpu.VMEM((LEAVES, 2 * VECS, 128), jnp.bfloat16),
            pltpu.VMEM((LEAVES, 2 * VECS, 128), jnp.bfloat16),
            pltpu.VMEM((3 * LEAVES + 8, VECS, 128), f32),
            pltpu.SemaphoreType.DMA((6,)),
            pltpu.SemaphoreType.DMA((3,)),
            pltpu.SemaphoreType.DMA((CHUNKS,)),
        ],
        compiler_params=pltpu.CompilerParams(vmem_limit_bytes=38 * 2**20),
        cost_estimate=pl.CostEstimate(flops=10_000_000_000, bytes_accessed=30_000_000, transcendentals=0),
        name="near",
    )(
        tile_count,
        in_hbm(tile_rows),
        in_hbm(tile_cols),
        in_hbm(adjoint),
        in_hbm(near_tiles),
        in_hbm(row_basis),
        in_hbm(by_leaf(leaf_lift)),
        spread_table,
        coupling_table,
        admissible_table,
    )
    gathered = lax.all_to_all(payload, AXES, 0, 0, tiled=True)
    across = [(i, (i + 1) % DEVICES) for i in range(1, DEVICES, 2)]
    far = lax.ppermute(far, AXES, across + [(b, a) for a, b in across])
    within = [(i, i ^ 1) for i in range(DEVICES)]
    chip = lax.ppermute(chip, AXES, within)

    wide, weights = pl.pallas_call(
        widen_kernel,
        out_shape=(
            jax.ShapeDtypeStruct((3, RANK, RANK, 128), f32),
            pltpu.HBM((2 * RANK, 24 * RANK), jnp.bfloat16),
        ),
        in_specs=[HBM, VMEM, HBM, HBM, HBM],
        out_specs=(VMEM, HBM),
        scratch_shapes=[
            pltpu.VMEM((2 * RANK, 24 * RANK), jnp.bfloat16),
            pltpu.VMEM((RANK, RANK, LEAVES), f32),
            pltpu.VMEM((RANK, RANK, 254), f32),
            pltpu.VMEM((4, RANK, RANK, 254), f32),
            pltpu.VMEM((4, 254), jnp.int32),
            pltpu.VMEM((5 * RANK, 8, RANK), f32),
            pltpu.SemaphoreType.DMA((5,)),
        ],
        compiler_params=pltpu.CompilerParams(vmem_limit_bytes=12 * 2**20),
        cost_estimate=pl.CostEstimate(flops=1_000_000_000, bytes_accessed=3_000_000, transcendentals=0),
        name="widen",
    )(
        in_hbm(by_leaf(leaf_spread)),
        weights,
        spread_table,
        coupling_table,
        admissible_table,
    )
    down = pl.pallas_call(
        tree_kernel,
        out_shape=jax.ShapeDtypeStruct((RANK, 128), f32),
        in_specs=[VMEM, HBM, VMEM],
        out_specs=VMEM,
        scratch_shapes=[
            pltpu.VMEM((RANK, VECS, 128), f32),
            pltpu.VMEM((RANK, VECS, 128), f32),
            pltpu.VMEM((24 * RANK, 256), jnp.bfloat16),
            pltpu.VMEM((2 * RANK, 24 * RANK), jnp.bfloat16),
            pltpu.SemaphoreType.DMA,
        ],
        compiler_params=pltpu.CompilerParams(vmem_limit_bytes=8 * 2**20),
        cost_estimate=pl.CostEstimate(flops=4_000_000_000, bytes_accessed=6_000_000, transcendentals=0),
        name="tree",
    )(gathered, in_hbm(weights), by_leaf(tree_lift))
    out = pl.pallas_call(
        final_kernel,
        out_shape=window,
        in_specs=[VMEM] * 6,
        out_specs=VMEM,
        compiler_params=pltpu.CompilerParams(vmem_limit_bytes=8 * 2**20),
        cost_estimate=pl.CostEstimate(flops=100_000_000, bytes_accessed=3_000_000, transcendentals=0),
        name="final",
    )(down, wide, column_basis, own, chip, far)
    return out.transpose(1, 0, 2).reshape(VECS, LEAVES * 128)


def solution(mesh):
    part = P(AXES, None, None)
    return jax.shard_map(
        local,
        mesh=mesh,
        in_specs=(P(None, AXES), part, P(AXES), P(AXES), P(AXES), part, part, part, part, P(), P(), P(), P()),
        out_specs=P(None, AXES),
        check_vma=False,
    )
```

```python
import functools

import jax
import jax.numpy as jnp
from jax import lax
from jax.experimental import pallas as pl
from jax.experimental.pallas import tpu as pltpu
from jax.sharding import PartitionSpec as P

AXES = ("leaf", "dom")
OFFSETS = (-3, -2, 2, 3)
DEVICES = 128
LEAVES = 40
TILES = 640
RANK = 32
VECS = 8
CHUNK = 64
CHUNKS = TILES // CHUNK
GROUP_BASES = (0, 16, 32)

VMEM = pl.BlockSpec(memory_space=pltpu.VMEM)
SMEM = pl.BlockSpec(memory_space=pltpu.SMEM)
HBM = pl.BlockSpec(memory_space=pltpu.HBM)


def lanes(shape):
    return lax.broadcasted_iota(jnp.int32, shape, 1)


def sublanes(shape):
    return lax.broadcasted_iota(jnp.int32, shape, 0)


def split(value):
    high = value.astype(jnp.bfloat16)
    low = (value - high.astype(jnp.float32)).astype(jnp.bfloat16)
    return high, low


def fill_expanded(matrices_ref, wide_ref):
    flat = matrices_ref[...].reshape(RANK * RANK, LEAVES)
    high, low = split(flat)
    for group, base in enumerate(GROUP_BASES):
        pick = (sublanes((LEAVES, 128)) == base + lanes((LEAVES, 128)) // VECS).astype(jnp.bfloat16)
        wide = jnp.dot(high, pick, preferred_element_type=jnp.float32)
        wide = wide + jnp.dot(low, pick, preferred_element_type=jnp.float32)
        wide_ref[group] = wide.reshape(RANK, RANK, 128)


def copies(pairs, sems):
    started = [pltpu.make_async_copy(source, target, sems.at[i]) for i, (source, target) in enumerate(pairs)]
    for one in started:
        one.start()
    return started


def gather_leaves(adjoint_ref, basis_ref, lift_ref, wide_ref, coef_ref, staged):
    fill_expanded(lift_ref, wide_ref)
    lane = lanes((RANK, 128)) // VECS
    total = jnp.zeros((RANK, 128), jnp.float32)
    for group, base in enumerate(GROUP_BASES):
        count = min(16, LEAVES - base)
        stacked = [
            adjoint_ref[:, (base + c) * 128 : (base + c + 1) * 128].astype(jnp.float32) for c in range(count)
        ]
        stacked += [jnp.zeros((VECS, 128), jnp.float32)] * (16 - count)
        vectors = jnp.concatenate(stacked, axis=0).astype(jnp.bfloat16)
        basis = basis_ref[base : base + count].reshape(count * RANK, 128)
        product = lax.dot_general(
            basis, vectors, (((1,), (1,)), ((), ())), preferred_element_type=jnp.float32
        )
        coefs = jnp.zeros((RANK, 128), jnp.float32)
        for c in range(count):
            coefs = jnp.where(lane == c, product[c * RANK : (c + 1) * RANK], coefs)
        coef_ref[...] = coefs
        for k in range(RANK):
            total = total + coef_ref[k : k + 1, :] * wide_ref[group, k]
    for shift in (8, 16, 32, 64):
        total = total + pltpu.roll(total, shift, 1)
    diagonal = lanes((16, 128)) // VECS == sublanes((16, 128))
    first = jnp.sum(jnp.where(diagonal, total[:16], 0.0), axis=0, keepdims=True)
    second = jnp.sum(jnp.where(diagonal, total[16:], 0.0), axis=0, keepdims=True)
    even = sublanes((2 * DEVICES, 128)) % 2 == 0
    staged[...] = jnp.where(even, first, second)


def contract(left, right):
    dims = (((1,), (1,)), ((), ()))
    high, low = split(left)
    other, rest = split(right)
    count = left.shape[0]
    both = lax.dot_general(jnp.concatenate([high, low], axis=0), other, dims, preferred_element_type=jnp.float32)
    last = lax.dot_general(high, rest, dims, preferred_element_type=jnp.float32)
    return both[:count] + both[count:] + last


def gather_lanes(value, index):
    return jnp.take_along_axis(value, index, axis=1)


def own_position():
    return lax.axis_index("leaf") * lax.axis_size("dom") + lax.axis_index("dom")


def works_late():
    leaf, dom = lax.axis_index("leaf"), lax.axis_index("dom")
    return 4 * (leaf // 4) + 8 * (leaf % 4) + 5 * (dom // 2) >= 30


def weigh(spread_ref, coupling_ref, admissible_ref, weight_out, pieces):
    position = own_position()
    row, column = sublanes((8, 254)), lanes((8, 254))
    base = 256 - lax.shift_right_logical(jnp.full((8, 254), 256, jnp.int32), row)
    mine = base + lax.shift_right_logical(jnp.full((8, 254), position, jnp.int32), row)
    pick = ((column == mine) & (row < 6)).astype(jnp.bfloat16)
    dims = (((1,), (1,)), ((), ()))

    def extract(values, first):
        high, low = split(values.reshape(RANK * RANK, 254))
        rows = lax.dot_general(pick, high, dims, preferred_element_type=jnp.float32)
        rows = rows + lax.dot_general(pick, low, dims, preferred_element_type=jnp.float32)
        for k in range(RANK):
            pieces[first + k] = rows[:, k * RANK : (k + 1) * RANK]

    extract(spread_ref[...], 4 * RANK)
    for slot in range(4):
        extract(coupling_ref[slot], slot * RANK)

    flags = jnp.concatenate([admissible_ref[...].astype(jnp.float32), jnp.zeros((4, 254), jnp.float32)], axis=0)
    flags = lax.dot_general(pick, flags.astype(jnp.bfloat16), dims, preferred_element_type=jnp.float32)
    slot = lanes((8, 128)) // RANK
    wider = (lanes((8, 128)) // RANK == sublanes((8, 128))).astype(jnp.bfloat16)
    flags = jnp.dot(flags.astype(jnp.bfloat16), wider, preferred_element_type=jnp.float32)
    level = sublanes((8, 128))
    other = lax.shift_right_logical(jnp.full((8, 128), position, jnp.int32), level)
    other = other + jnp.where(slot < 2, slot - 3, slot)
    size = lax.shift_right_logical(jnp.full((8, 128), DEVICES, jnp.int32), level)
    flags = jnp.where((other >= 0) & (other < size), flags, 0.0)
    square = (RANK, RANK)
    path = (sublanes(square) == lanes(square)).astype(jnp.float32)
    for height in range(6):
        if height:
            path = contract(path, pieces[4 * RANK : 5 * RANK, height - 1, :])
        allowed = flags[height : height + 1]
        high, low = split(contract(path, pieces[: 4 * RANK, height, :]) * allowed)
        weight_out[:RANK, height * 128 : (height + 1) * 128] = high
        weight_out[RANK:, height * 128 : (height + 1) * 128] = low


def widen_kernel(
    leaf_spread_hbm,
    early_ref,
    spread_hbm,
    coupling_hbm,
    admissible_hbm,
    wide_out,
    weight_out,
    weight_ref,
    leaf_spread_ref,
    spread_ref,
    coupling_ref,
    admissible_ref,
    pieces,
    sems,
):
    late = works_late()
    leaf_spreads = pltpu.make_async_copy(leaf_spread_hbm, leaf_spread_ref, sems.at[3])
    leaf_spreads.start()

    @pl.when(late)
    def _():
        copies(
            [(spread_hbm, spread_ref), (coupling_hbm, coupling_ref), (admissible_hbm, admissible_ref)], sems
        )

    leaf_spreads.wait()
    fill_expanded(leaf_spread_ref, wide_out)

    @pl.when(late)
    def _():
        pltpu.make_async_copy(spread_hbm, spread_ref, sems.at[0]).wait()
        pltpu.make_async_copy(coupling_hbm, coupling_ref, sems.at[1]).wait()
        pltpu.make_async_copy(admissible_hbm, admissible_ref, sems.at[2]).wait()
        weigh(spread_ref, coupling_ref, admissible_ref, weight_ref, pieces)

    @pl.when(jnp.logical_not(late))
    def _():
        weight_ref[...] = early_ref[...]

    write = pltpu.make_async_copy(weight_ref, weight_out, sems.at[4])
    write.start()
    write.wait()


def near_kernel(
    count_ref,
    rows_hbm,
    cols_hbm,
    adjoint_hbm,
    tiles_ref,
    basis_hbm,
    leaf_lift_hbm,
    spread_hbm,
    coupling_hbm,
    admissible_hbm,
    payload_out,
    weight_out,
    own_ref,
    chip_ref,
    far_ref,
    rows_ref,
    cols_ref,
    adjoint_ref,
    basis_ref,
    leaf_lift_ref,
    spread_ref,
    coupling_ref,
    admissible_ref,
    pieces,
    wide_ref,
    coef_ref,
    staged,
    buffer,
    uppers,
    lowers,
    sums,
    small_sems,
    table_sems,
    sems,
):
    early = jnp.logical_not(works_late())
    tables = [(spread_hbm, spread_ref), (coupling_hbm, coupling_ref), (admissible_hbm, admissible_ref)]
    arriving = copies(
        [
            (leaf_lift_hbm, leaf_lift_ref),
            (basis_hbm, basis_ref),
            (adjoint_hbm, adjoint_ref),
            (rows_hbm, rows_ref),
            (cols_hbm, cols_ref),
        ],
        small_sems,
    )

    @pl.when(early)
    def _():
        copies(tables, table_sems)

    used = count_ref[0]
    chunks = lax.div(used + (CHUNK - 1), CHUNK)

    def copy(c):
        part = pl.ds(c * CHUNK, CHUNK)
        return pltpu.make_async_copy(tiles_ref.at[part], buffer.at[part], sems.at[c])

    def start(c, carry):
        copy(c).start()
        return carry

    lax.fori_loop(0, chunks, start, 0)
    sums[...] = jnp.zeros_like(sums)
    for one in arriving:
        one.wait()
    blank = jnp.zeros((VECS, 128), jnp.float32)
    for c in range(LEAVES):
        vectors = adjoint_ref[:, c * 128 : (c + 1) * 128].astype(jnp.float32)
        uppers[c] = jnp.concatenate([vectors, blank], axis=0).astype(jnp.bfloat16)
        lowers[c] = jnp.concatenate([blank, vectors], axis=0).astype(jnp.bfloat16)
    gather_leaves(adjoint_ref, basis_ref, leaf_lift_ref, wide_ref, coef_ref, staged)
    write = pltpu.make_async_copy(staged, payload_out, small_sems.at[5])
    write.start()

    @pl.when(early)
    def _():
        for i, (source, target) in enumerate(tables):
            pltpu.make_async_copy(source, target, table_sems.at[i]).wait()
        weigh(spread_ref, coupling_ref, admissible_ref, weight_out, pieces)

    def body(c, carry):
        copy(c).wait()
        first = c * CHUNK
        products = []
        for j in range(0, CHUNK, 2):
            left = jnp.concatenate([uppers[rows_ref[first + j]], lowers[rows_ref[first + j + 1]]], axis=1)
            right = buffer[pl.ds(first + j, 2)].reshape(256, 128)
            both = jnp.dot(left, right, preferred_element_type=jnp.float32)
            products += [both[:VECS], both[VECS:]]
        for j in range(CHUNK):
            target = jnp.where(first + j < used, cols_ref[first + j], 3 * LEAVES)
            sums[target] = sums[target] + products[j]
        return carry

    lax.fori_loop(0, chunks, body, 0)
    write.wait()
    odd = lax.rem(lax.axis_index("dom"), 2)
    own_ref[...] = sums[LEAVES : 2 * LEAVES]
    chip_ref[...] = sums[pl.ds((1 - odd) * 2 * LEAVES, LEAVES)]
    position = own_position()
    inside = (position > 0) & (position < DEVICES - 1)
    far_ref[...] = jnp.where(inside, sums[pl.ds(odd * 2 * LEAVES, LEAVES)], 0.0)


def lift_level(row, count, matrix, inner_steps=4):
    def body(step, totals):
        for inner in range(inner_steps):
            k = step * inner_steps + inner
            values = matrix(k)
            totals = tuple(totals[r] + row(k, r) * values for r in range(count))
        return totals

    start = tuple(jnp.zeros((RANK, 128), jnp.float32) for _ in range(count))
    if inner_steps == RANK:
        return body(0, start)
    return lax.fori_loop(0, RANK // inner_steps, body, start)


def tree_kernel(gathered_ref, weight_hbm, lift_ref, down_ref, up0, up, partners, weight_ref, sem):
    weights = pltpu.make_async_copy(weight_hbm, weight_ref, sem)
    weights.start()
    position = own_position()
    lane = lanes((RANK, 128))
    vector = lane % VECS

    def put(height, slot, values):
        high, low = split(values)
        first = (height * 4 + slot) * RANK
        partners[first : first + RANK, :128] = high
        partners[first : first + RANK, 128:] = low

    def partner(height, offset):
        return jnp.clip((position >> height) + offset, 0, (DEVICES >> height) - 1)

    for half in range(2):
        block = gathered_ref[pl.ds(half, DEVICES, stride=2), :].T
        up0[half * 16 : (half + 1) * 16] = block.reshape(16, VECS, 128)
    spot = sublanes((16, 128)) * VECS + lanes((16, 128)) % VECS
    for slot, offset in enumerate(OFFSETS):
        rows = gathered_ref[pl.ds(2 * partner(0, offset), 2), :]
        halves = [gather_lanes(jnp.broadcast_to(rows[i : i + 1], (16, 128)), spot) for i in range(2)]
        put(0, slot, jnp.concatenate(halves, axis=0))

    level = lift_level(lambda k, r: up0[k, r : r + 1, :], VECS, lambda k: lift_ref[k, :, :128], 16)
    for height in range(1, 6):
        nodes = DEVICES >> height
        width = max(nodes, 16)
        paired = [values + pltpu.roll(values, 127, 1) for values in level]
        if height <= 3:
            index = lane // (2 * width) * (2 * width) + 2 * (lane % width)
            if height == 1:
                index = 2 * (lane % 64)
            count = len(paired) // 2
            second = (lane // width) % 2 == 1
            level = [
                jnp.where(second, gather_lanes(paired[r + count], index), gather_lanes(paired[r], index))
                for r in range(count)
            ]
        else:
            count = 1
            level = [gather_lanes(paired[0], lane // 16 * 16 + 2 * (lane % nodes))]
        for slot, offset in enumerate(OFFSETS):
            place = vector // count * width + partner(height, offset)
            chosen = gather_lanes(level[0], place)
            for r in range(1, count):
                chosen = jnp.where(vector % count == r, gather_lanes(level[r], place), chosen)
            put(height, slot, chosen)
        if height < 5:
            for r in range(count):
                up[r] = level[r]
            spot = 128 - (256 >> height) + lane % nodes

            def repeated(k, spot=spot):
                tail = jnp.concatenate([lift_ref[k, :, 128:254], jnp.zeros((RANK, 2), jnp.float32)], axis=1)
                return gather_lanes(tail, spot)

            level = lift_level(lambda k, r: up[r, k : k + 1, :], count, repeated, RANK)

    weights.wait()
    product = jnp.dot(weight_ref[...], partners[...], preferred_element_type=jnp.float32)
    down_ref[...] = product[:RANK, :128] + product[:RANK, 128:] + product[RANK:, :128]


def final_kernel(down, wide_ref, basis_ref, own_ref, chip_ref, far_ref, out_ref):
    square = lanes((128, 128)) // RANK == (sublanes((128, 128)) // VECS) % 4
    for group, base in enumerate(GROUP_BASES):
        count = min(16, LEAVES - base)
        total = jnp.zeros((RANK, 128), jnp.float32)
        for k in range(RANK):
            total = total + down[k : k + 1, :] * wide_ref[group, k]
        values = jnp.where(square, jnp.concatenate([total] * 4, axis=0).T, 0.0)
        for quad in range(count // 4):
            high, low = split(values[quad * 32 : (quad + 1) * 32])
            leaf = base + quad * 4
            matrix = basis_ref[leaf : leaf + 4].reshape(128, 128)
            both = jnp.dot(jnp.concatenate([high, low], axis=0), matrix, preferred_element_type=jnp.float32)
            part = slice(leaf, leaf + 4)
            near = own_ref[part] + (chip_ref[part] + far_ref[part])
            out_ref[part] = near + (both[:32] + both[32:]).reshape(4, VECS, 128)


def local(
    adjoint,
    near_tiles,
    tile_rows,
    tile_cols,
    tile_count,
    row_basis,
    column_basis,
    leaf_lift,
    leaf_spread,
    tree_lift,
    tree_spread,
    coupling,
    admissible,
):
    f32 = jnp.float32
    by_leaf = lambda x: jnp.transpose(x, (1, 2, 0))
    in_hbm = lambda x: pltpu.with_memory_space_constraint(x, pltpu.HBM)
    window = jax.ShapeDtypeStruct((LEAVES, VECS, 128), f32)
    spread_table = in_hbm(by_leaf(tree_spread))
    coupling_table = in_hbm(jnp.transpose(coupling, (1, 2, 3, 0)))
    admissible_table = in_hbm(admissible.T)
    payload, weights, own, chip, far = pl.pallas_call(
        near_kernel,
        out_shape=(
            pltpu.HBM((2 * DEVICES, 128), f32),
            jax.ShapeDtypeStruct((2 * RANK, 24 * RANK), jnp.bfloat16),
            window,
            window,
            window,
        ),
        in_specs=[SMEM] + [HBM] * 9,
        out_specs=(HBM, VMEM, VMEM, VMEM, VMEM),
        scratch_shapes=[
            pltpu.SMEM((TILES,), jnp.int32),
            pltpu.SMEM((TILES,), jnp.int32),
            pltpu.VMEM((VECS, LEAVES * 128), jnp.bfloat16),
            pltpu.VMEM((LEAVES, RANK, 128), jnp.bfloat16),
            pltpu.VMEM((RANK, RANK, LEAVES), f32),
            pltpu.VMEM((RANK, RANK, 254), f32),
            pltpu.VMEM((4, RANK, RANK, 254), f32),
            pltpu.VMEM((4, 254), jnp.int32),
            pltpu.VMEM((5 * RANK, 8, RANK), f32),
            pltpu.VMEM((3, RANK, RANK, 128), f32),
            pltpu.VMEM((RANK, 128), f32),
            pltpu.VMEM((2 * DEVICES, 128), f32),
            pltpu.VMEM((TILES, 128, 128), jnp.bfloat16),
            pltpu.VMEM((LEAVES, 2 * VECS, 128), jnp.bfloat16),
            pltpu.VMEM((LEAVES, 2 * VECS, 128), jnp.bfloat16),
            pltpu.VMEM((3 * LEAVES + 8, VECS, 128), f32),
            pltpu.SemaphoreType.DMA((6,)),
            pltpu.SemaphoreType.DMA((3,)),
            pltpu.SemaphoreType.DMA((CHUNKS,)),
        ],
        compiler_params=pltpu.CompilerParams(vmem_limit_bytes=38 * 2**20),
        cost_estimate=pl.CostEstimate(flops=10_000_000_000, bytes_accessed=30_000_000, transcendentals=0),
        name="near",
    )(
        tile_count,
        in_hbm(tile_rows),
        in_hbm(tile_cols),
        in_hbm(adjoint),
        in_hbm(near_tiles),
        in_hbm(row_basis),
        in_hbm(by_leaf(leaf_lift)),
        spread_table,
        coupling_table,
        admissible_table,
    )
    gathered = lax.all_to_all(payload, AXES, 0, 0, tiled=True)
    across = [(i, (i + 1) % DEVICES) for i in range(1, DEVICES, 2)]
    far = lax.ppermute(far, AXES, across + [(b, a) for a, b in across])
    within = [(i, i ^ 1) for i in range(DEVICES)]
    chip = lax.ppermute(chip, AXES, within)

    wide, weights = pl.pallas_call(
        widen_kernel,
        out_shape=(
            jax.ShapeDtypeStruct((3, RANK, RANK, 128), f32),
            pltpu.HBM((2 * RANK, 24 * RANK), jnp.bfloat16),
        ),
        in_specs=[HBM, VMEM, HBM, HBM, HBM],
        out_specs=(VMEM, HBM),
        scratch_shapes=[
            pltpu.VMEM((2 * RANK, 24 * RANK), jnp.bfloat16),
            pltpu.VMEM((RANK, RANK, LEAVES), f32),
            pltpu.VMEM((RANK, RANK, 254), f32),
            pltpu.VMEM((4, RANK, RANK, 254), f32),
            pltpu.VMEM((4, 254), jnp.int32),
            pltpu.VMEM((5 * RANK, 8, RANK), f32),
            pltpu.SemaphoreType.DMA((5,)),
        ],
        compiler_params=pltpu.CompilerParams(vmem_limit_bytes=12 * 2**20),
        cost_estimate=pl.CostEstimate(flops=1_000_000_000, bytes_accessed=3_000_000, transcendentals=0),
        name="widen",
    )(
        in_hbm(by_leaf(leaf_spread)),
        weights,
        spread_table,
        coupling_table,
        admissible_table,
    )
    down = pl.pallas_call(
        tree_kernel,
        out_shape=jax.ShapeDtypeStruct((RANK, 128), f32),
        in_specs=[VMEM, HBM, VMEM],
        out_specs=VMEM,
        scratch_shapes=[
            pltpu.VMEM((RANK, VECS, 128), f32),
            pltpu.VMEM((4, RANK, 128), f32),
            pltpu.VMEM((24 * RANK, 256), jnp.bfloat16),
            pltpu.VMEM((2 * RANK, 24 * RANK), jnp.bfloat16),
            pltpu.SemaphoreType.DMA,
        ],
        compiler_params=pltpu.CompilerParams(vmem_limit_bytes=8 * 2**20),
        cost_estimate=pl.CostEstimate(flops=4_000_000_000, bytes_accessed=6_000_000, transcendentals=0),
        name="tree",
    )(gathered, in_hbm(weights), by_leaf(tree_lift))
    out = pl.pallas_call(
        final_kernel,
        out_shape=window,
        in_specs=[VMEM] * 6,
        out_specs=VMEM,
        compiler_params=pltpu.CompilerParams(vmem_limit_bytes=8 * 2**20),
        cost_estimate=pl.CostEstimate(flops=100_000_000, bytes_accessed=3_000_000, transcendentals=0),
        name="final",
    )(down, wide, column_basis, own, chip, far)
    return out.transpose(1, 0, 2).reshape(VECS, LEAVES * 128)


def solution(mesh):
    part = P(AXES, None, None)
    return jax.shard_map(
        local,
        mesh=mesh,
        in_specs=(P(None, AXES), part, P(AXES), P(AXES), P(AXES), part, part, part, part, P(), P(), P(), P()),
        out_specs=P(None, AXES),
        check_vma=False,
    )
```

```python
import functools

import jax
import jax.numpy as jnp
from jax import lax
from jax.experimental import pallas as pl
from jax.experimental.pallas import tpu as pltpu
from jax.sharding import PartitionSpec as P

AXES = ("leaf", "dom")
OFFSETS = (-3, -2, 2, 3)
DEVICES = 128
LEAVES = 40
TILES = 640
RANK = 32
VECS = 8
CHUNK = 64
CHUNKS = TILES // CHUNK
GROUP_BASES = (0, 16, 32)

VMEM = pl.BlockSpec(memory_space=pltpu.VMEM)
SMEM = pl.BlockSpec(memory_space=pltpu.SMEM)
HBM = pl.BlockSpec(memory_space=pltpu.HBM)


def lanes(shape):
    return lax.broadcasted_iota(jnp.int32, shape, 1)


def sublanes(shape):
    return lax.broadcasted_iota(jnp.int32, shape, 0)


def split(value):
    high = value.astype(jnp.bfloat16)
    low = (value - high.astype(jnp.float32)).astype(jnp.bfloat16)
    return high, low


def fill_expanded(matrices_ref, wide_ref):
    flat = matrices_ref[...].reshape(RANK * RANK, LEAVES)
    high, low = split(flat)
    for group, base in enumerate(GROUP_BASES):
        pick = (sublanes((LEAVES, 128)) == base + lanes((LEAVES, 128)) // VECS).astype(jnp.bfloat16)
        wide = jnp.dot(high, pick, preferred_element_type=jnp.float32)
        wide = wide + jnp.dot(low, pick, preferred_element_type=jnp.float32)
        wide_ref[group] = wide.reshape(RANK, RANK, 128)


def copies(pairs, sems):
    started = [pltpu.make_async_copy(source, target, sems.at[i]) for i, (source, target) in enumerate(pairs)]
    for one in started:
        one.start()
    return started


def gather_leaves(adjoint_ref, basis_ref, lift_ref, wide_ref, coef_ref, staged):
    fill_expanded(lift_ref, wide_ref)
    lane = lanes((RANK, 128)) // VECS
    total = jnp.zeros((RANK, 128), jnp.float32)
    for group, base in enumerate(GROUP_BASES):
        count = min(16, LEAVES - base)
        stacked = [
            adjoint_ref[:, (base + c) * 128 : (base + c + 1) * 128].astype(jnp.float32) for c in range(count)
        ]
        stacked += [jnp.zeros((VECS, 128), jnp.float32)] * (16 - count)
        vectors = jnp.concatenate(stacked, axis=0).astype(jnp.bfloat16)
        basis = basis_ref[base : base + count].reshape(count * RANK, 128)
        product = lax.dot_general(
            basis, vectors, (((1,), (1,)), ((), ())), preferred_element_type=jnp.float32
        )
        coefs = jnp.zeros((RANK, 128), jnp.float32)
        for c in range(count):
            coefs = jnp.where(lane == c, product[c * RANK : (c + 1) * RANK], coefs)
        coef_ref[...] = coefs
        for k in range(RANK):
            total = total + coef_ref[k : k + 1, :] * wide_ref[group, k]
    for shift in (8, 16, 32, 64):
        total = total + pltpu.roll(total, shift, 1)
    diagonal = lanes((16, 128)) // VECS == sublanes((16, 128))
    first = jnp.sum(jnp.where(diagonal, total[:16], 0.0), axis=0, keepdims=True)
    second = jnp.sum(jnp.where(diagonal, total[16:], 0.0), axis=0, keepdims=True)
    even = sublanes((2 * DEVICES, 128)) % 2 == 0
    staged[...] = jnp.where(even, first, second)


def contract(left, right):
    dims = (((1,), (1,)), ((), ()))
    high, low = split(left)
    other, rest = split(right)
    count = left.shape[0]
    both = lax.dot_general(jnp.concatenate([high, low], axis=0), other, dims, preferred_element_type=jnp.float32)
    last = lax.dot_general(high, rest, dims, preferred_element_type=jnp.float32)
    return both[:count] + both[count:] + last


def gather_lanes(value, index):
    return jnp.take_along_axis(value, index, axis=1)


def own_position():
    return lax.axis_index("leaf") * lax.axis_size("dom") + lax.axis_index("dom")


def works_late():
    leaf, dom = lax.axis_index("leaf"), lax.axis_index("dom")
    return 4 * (leaf // 4) + 8 * (leaf % 4) + 5 * (dom // 2) >= 30


def weigh(spread_ref, coupling_ref, admissible_ref, weight_out, pieces):
    position = own_position()
    row, column = sublanes((8, 254)), lanes((8, 254))
    base = 256 - lax.shift_right_logical(jnp.full((8, 254), 256, jnp.int32), row)
    mine = base + lax.shift_right_logical(jnp.full((8, 254), position, jnp.int32), row)
    pick = ((column == mine) & (row < 6)).astype(jnp.bfloat16)
    dims = (((1,), (1,)), ((), ()))

    def extract(values, first):
        high, low = split(values.reshape(RANK * RANK, 254))
        rows = lax.dot_general(pick, high, dims, preferred_element_type=jnp.float32)
        rows = rows + lax.dot_general(pick, low, dims, preferred_element_type=jnp.float32)
        for k in range(RANK):
            pieces[first + k] = rows[:, k * RANK : (k + 1) * RANK]

    extract(spread_ref[...], 4 * RANK)
    for slot in range(4):
        extract(coupling_ref[slot], slot * RANK)

    flags = jnp.concatenate([admissible_ref[...].astype(jnp.float32), jnp.zeros((4, 254), jnp.float32)], axis=0)
    flags = lax.dot_general(pick, flags.astype(jnp.bfloat16), dims, preferred_element_type=jnp.float32)
    slot = lanes((8, 128)) // RANK
    wider = (lanes((8, 128)) // RANK == sublanes((8, 128))).astype(jnp.bfloat16)
    flags = jnp.dot(flags.astype(jnp.bfloat16), wider, preferred_element_type=jnp.float32)
    level = sublanes((8, 128))
    other = lax.shift_right_logical(jnp.full((8, 128), position, jnp.int32), level)
    other = other + jnp.where(slot < 2, slot - 3, slot)
    size = lax.shift_right_logical(jnp.full((8, 128), DEVICES, jnp.int32), level)
    flags = jnp.where((other >= 0) & (other < size), flags, 0.0)
    square = (RANK, RANK)
    path = (sublanes(square) == lanes(square)).astype(jnp.float32)
    for height in range(6):
        if height:
            path = contract(path, pieces[4 * RANK : 5 * RANK, height - 1, :])
        allowed = flags[height : height + 1]
        high, low = split(contract(path, pieces[: 4 * RANK, height, :]) * allowed)
        weight_out[:RANK, height * 128 : (height + 1) * 128] = high
        weight_out[RANK:, height * 128 : (height + 1) * 128] = low


def widen_kernel(
    leaf_spread_hbm,
    early_ref,
    spread_hbm,
    coupling_hbm,
    admissible_hbm,
    wide_out,
    weight_out,
    weight_ref,
    leaf_spread_ref,
    spread_ref,
    coupling_ref,
    admissible_ref,
    pieces,
    sems,
):
    late = works_late()
    leaf_spreads = pltpu.make_async_copy(leaf_spread_hbm, leaf_spread_ref, sems.at[3])
    leaf_spreads.start()

    @pl.when(late)
    def _():
        copies(
            [(spread_hbm, spread_ref), (coupling_hbm, coupling_ref), (admissible_hbm, admissible_ref)], sems
        )

    leaf_spreads.wait()
    fill_expanded(leaf_spread_ref, wide_out)

    @pl.when(late)
    def _():
        pltpu.make_async_copy(spread_hbm, spread_ref, sems.at[0]).wait()
        pltpu.make_async_copy(coupling_hbm, coupling_ref, sems.at[1]).wait()
        pltpu.make_async_copy(admissible_hbm, admissible_ref, sems.at[2]).wait()
        weigh(spread_ref, coupling_ref, admissible_ref, weight_ref, pieces)

    @pl.when(jnp.logical_not(late))
    def _():
        weight_ref[...] = early_ref[...]

    write = pltpu.make_async_copy(weight_ref, weight_out, sems.at[4])
    write.start()
    write.wait()


def near_kernel(
    count_ref,
    rows_hbm,
    cols_hbm,
    adjoint_hbm,
    tiles_ref,
    basis_hbm,
    leaf_lift_hbm,
    spread_hbm,
    coupling_hbm,
    admissible_hbm,
    payload_out,
    weight_out,
    own_ref,
    chip_ref,
    far_ref,
    rows_ref,
    cols_ref,
    adjoint_ref,
    basis_ref,
    leaf_lift_ref,
    spread_ref,
    coupling_ref,
    admissible_ref,
    pieces,
    wide_ref,
    coef_ref,
    staged,
    buffer,
    uppers,
    lowers,
    sums,
    small_sems,
    table_sems,
    sems,
):
    early = jnp.logical_not(works_late())
    tables = [(spread_hbm, spread_ref), (coupling_hbm, coupling_ref), (admissible_hbm, admissible_ref)]
    arriving = copies(
        [
            (leaf_lift_hbm, leaf_lift_ref),
            (basis_hbm, basis_ref),
            (adjoint_hbm, adjoint_ref),
            (rows_hbm, rows_ref),
            (cols_hbm, cols_ref),
        ],
        small_sems,
    )

    @pl.when(early)
    def _():
        copies(tables, table_sems)

    used = count_ref[0]
    chunks = lax.div(used + (CHUNK - 1), CHUNK)

    def copy(c):
        part = pl.ds(c * CHUNK, CHUNK)
        return pltpu.make_async_copy(tiles_ref.at[part], buffer.at[part], sems.at[c])

    def start(c, carry):
        copy(c).start()
        return carry

    lax.fori_loop(0, chunks, start, 0)
    sums[...] = jnp.zeros_like(sums)
    for one in arriving:
        one.wait()
    blank = jnp.zeros((VECS, 128), jnp.float32)
    for c in range(LEAVES):
        vectors = adjoint_ref[:, c * 128 : (c + 1) * 128].astype(jnp.float32)
        uppers[c] = jnp.concatenate([vectors, blank], axis=0).astype(jnp.bfloat16)
        lowers[c] = jnp.concatenate([blank, vectors], axis=0).astype(jnp.bfloat16)
    gather_leaves(adjoint_ref, basis_ref, leaf_lift_ref, wide_ref, coef_ref, staged)
    write = pltpu.make_async_copy(staged, payload_out, small_sems.at[5])
    write.start()

    @pl.when(early)
    def _():
        for i, (source, target) in enumerate(tables):
            pltpu.make_async_copy(source, target, table_sems.at[i]).wait()
        weigh(spread_ref, coupling_ref, admissible_ref, weight_out, pieces)

    def body(c, carry):
        copy(c).wait()
        first = c * CHUNK
        products = []
        for j in range(0, CHUNK, 2):
            left = jnp.concatenate([uppers[rows_ref[first + j]], lowers[rows_ref[first + j + 1]]], axis=1)
            right = buffer[pl.ds(first + j, 2)].reshape(256, 128)
            both = jnp.dot(left, right, preferred_element_type=jnp.float32)
            products += [both[:VECS], both[VECS:]]
        for j in range(CHUNK):
            target = jnp.where(first + j < used, cols_ref[first + j], 3 * LEAVES)
            sums[target] = sums[target] + products[j]
        return carry

    lax.fori_loop(0, chunks, body, 0)
    write.wait()
    odd = lax.rem(lax.axis_index("dom"), 2)
    own_ref[...] = sums[LEAVES : 2 * LEAVES]
    chip_ref[...] = sums[pl.ds((1 - odd) * 2 * LEAVES, LEAVES)]
    position = own_position()
    inside = (position > 0) & (position < DEVICES - 1)
    far_ref[...] = jnp.where(inside, sums[pl.ds(odd * 2 * LEAVES, LEAVES)], 0.0)


def lift_level(row, count, matrix, inner_steps=4):
    def body(step, totals):
        for inner in range(inner_steps):
            k = step * inner_steps + inner
            values = matrix(k)
            totals = tuple(totals[r] + row(k, r) * values for r in range(count))
        return totals

    start = tuple(jnp.zeros((RANK, 128), jnp.float32) for _ in range(count))
    if inner_steps == RANK:
        parts = [list(start) for _ in range(4)]
        for k in range(RANK):
            values = matrix(k)
            part = parts[k % 4]
            for r in range(count):
                part[r] = part[r] + row(k, r) * values
        return tuple((parts[0][r] + parts[1][r]) + (parts[2][r] + parts[3][r]) for r in range(count))
    return lax.fori_loop(0, RANK // inner_steps, body, start)


def tree_kernel(gathered_ref, weight_hbm, lift_ref, down_ref, up0, up, partners, weight_ref, sem):
    weights = pltpu.make_async_copy(weight_hbm, weight_ref, sem)
    weights.start()
    position = own_position()
    lane = lanes((RANK, 128))
    vector = lane % VECS

    def put(height, slot, values):
        high, low = split(values)
        first = (height * 4 + slot) * RANK
        partners[first : first + RANK, :128] = high
        partners[first : first + RANK, 128:] = low

    def partner(height, offset):
        return jnp.clip((position >> height) + offset, 0, (DEVICES >> height) - 1)

    for half in range(2):
        block = gathered_ref[pl.ds(half, DEVICES, stride=2), :].T
        up0[half * 16 : (half + 1) * 16] = block.reshape(16, VECS, 128)
    spot = sublanes((16, 128)) * VECS + lanes((16, 128)) % VECS
    for slot, offset in enumerate(OFFSETS):
        rows = gathered_ref[pl.ds(2 * partner(0, offset), 2), :]
        halves = [gather_lanes(jnp.broadcast_to(rows[i : i + 1], (16, 128)), spot) for i in range(2)]
        put(0, slot, jnp.concatenate(halves, axis=0))

    level = lift_level(lambda k, r: up0[k, r : r + 1, :], VECS, lambda k: lift_ref[k, :, :128], 16)
    for height in range(1, 6):
        nodes = DEVICES >> height
        width = max(nodes, 16)
        paired = [values + pltpu.roll(values, 127, 1) for values in level]
        if height <= 3:
            index = lane // (2 * width) * (2 * width) + 2 * (lane % width)
            if height == 1:
                index = 2 * (lane % 64)
            count = len(paired) // 2
            second = (lane // width) % 2 == 1
            level = [
                jnp.where(second, gather_lanes(paired[r + count], index), gather_lanes(paired[r], index))
                for r in range(count)
            ]
        else:
            count = 1
            level = [gather_lanes(paired[0], lane // 16 * 16 + 2 * (lane % nodes))]
        for slot, offset in enumerate(OFFSETS):
            place = vector // count * width + partner(height, offset)
            chosen = gather_lanes(level[0], place)
            for r in range(1, count):
                chosen = jnp.where(vector % count == r, gather_lanes(level[r], place), chosen)
            put(height, slot, chosen)
        if height < 5:
            for r in range(count):
                up[r] = level[r]
            spot = 128 - (256 >> height) + lane % nodes

            def repeated(k, spot=spot):
                tail = jnp.concatenate([lift_ref[k, :, 128:254], jnp.zeros((RANK, 2), jnp.float32)], axis=1)
                return gather_lanes(tail, spot)

            level = lift_level(lambda k, r: up[r, k : k + 1, :], count, repeated, RANK)

    weights.wait()
    product = jnp.dot(weight_ref[...], partners[...], preferred_element_type=jnp.float32)
    down_ref[...] = product[:RANK, :128] + product[:RANK, 128:] + product[RANK:, :128]


def final_kernel(down, wide_ref, basis_ref, own_ref, chip_ref, far_ref, out_ref):
    square = lanes((128, 128)) // RANK == (sublanes((128, 128)) // VECS) % 4
    for group, base in enumerate(GROUP_BASES):
        count = min(16, LEAVES - base)
        parts = [jnp.zeros((RANK, 128), jnp.float32)] * 4
        for k in range(RANK):
            parts[k % 4] = parts[k % 4] + down[k : k + 1, :] * wide_ref[group, k]
        total = (parts[0] + parts[1]) + (parts[2] + parts[3])
        values = jnp.where(square, jnp.concatenate([total] * 4, axis=0).T, 0.0)
        for quad in range(count // 4):
            high, low = split(values[quad * 32 : (quad + 1) * 32])
            leaf = base + quad * 4
            matrix = basis_ref[leaf : leaf + 4].reshape(128, 128)
            both = jnp.dot(jnp.concatenate([high, low], axis=0), matrix, preferred_element_type=jnp.float32)
            part = slice(leaf, leaf + 4)
            near = own_ref[part] + (chip_ref[part] + far_ref[part])
            out_ref[part] = near + (both[:32] + both[32:]).reshape(4, VECS, 128)


def local(
    adjoint,
    near_tiles,
    tile_rows,
    tile_cols,
    tile_count,
    row_basis,
    column_basis,
    leaf_lift,
    leaf_spread,
    tree_lift,
    tree_spread,
    coupling,
    admissible,
):
    f32 = jnp.float32
    by_leaf = lambda x: jnp.transpose(x, (1, 2, 0))
    in_hbm = lambda x: pltpu.with_memory_space_constraint(x, pltpu.HBM)
    window = jax.ShapeDtypeStruct((LEAVES, VECS, 128), f32)
    spread_table = in_hbm(by_leaf(tree_spread))
    coupling_table = in_hbm(jnp.transpose(coupling, (1, 2, 3, 0)))
    admissible_table = in_hbm(admissible.T)
    payload, weights, own, chip, far = pl.pallas_call(
        near_kernel,
        out_shape=(
            pltpu.HBM((2 * DEVICES, 128), f32),
            jax.ShapeDtypeStruct((2 * RANK, 24 * RANK), jnp.bfloat16),
            window,
            window,
            window,
        ),
        in_specs=[SMEM] + [HBM] * 9,
        out_specs=(HBM, VMEM, VMEM, VMEM, VMEM),
        scratch_shapes=[
            pltpu.SMEM((TILES,), jnp.int32),
            pltpu.SMEM((TILES,), jnp.int32),
            pltpu.VMEM((VECS, LEAVES * 128), jnp.bfloat16),
            pltpu.VMEM((LEAVES, RANK, 128), jnp.bfloat16),
            pltpu.VMEM((RANK, RANK, LEAVES), f32),
            pltpu.VMEM((RANK, RANK, 254), f32),
            pltpu.VMEM((4, RANK, RANK, 254), f32),
            pltpu.VMEM((4, 254), jnp.int32),
            pltpu.VMEM((5 * RANK, 8, RANK), f32),
            pltpu.VMEM((3, RANK, RANK, 128), f32),
            pltpu.VMEM((RANK, 128), f32),
            pltpu.VMEM((2 * DEVICES, 128), f32),
            pltpu.VMEM((TILES, 128, 128), jnp.bfloat16),
            pltpu.VMEM((LEAVES, 2 * VECS, 128), jnp.bfloat16),
            pltpu.VMEM((LEAVES, 2 * VECS, 128), jnp.bfloat16),
            pltpu.VMEM((3 * LEAVES + 8, VECS, 128), f32),
            pltpu.SemaphoreType.DMA((6,)),
            pltpu.SemaphoreType.DMA((3,)),
            pltpu.SemaphoreType.DMA((CHUNKS,)),
        ],
        compiler_params=pltpu.CompilerParams(vmem_limit_bytes=38 * 2**20),
        cost_estimate=pl.CostEstimate(flops=10_000_000_000, bytes_accessed=30_000_000, transcendentals=0),
        name="near",
    )(
        tile_count,
        in_hbm(tile_rows),
        in_hbm(tile_cols),
        in_hbm(adjoint),
        in_hbm(near_tiles),
        in_hbm(row_basis),
        in_hbm(by_leaf(leaf_lift)),
        spread_table,
        coupling_table,
        admissible_table,
    )
    gathered = lax.all_to_all(payload, AXES, 0, 0, tiled=True)
    across = [(i, (i + 1) % DEVICES) for i in range(1, DEVICES, 2)]
    far = lax.ppermute(far, AXES, across + [(b, a) for a, b in across])
    within = [(i, i ^ 1) for i in range(DEVICES)]
    chip = lax.ppermute(chip, AXES, within)

    wide, weights = pl.pallas_call(
        widen_kernel,
        out_shape=(
            jax.ShapeDtypeStruct((3, RANK, RANK, 128), f32),
            pltpu.HBM((2 * RANK, 24 * RANK), jnp.bfloat16),
        ),
        in_specs=[HBM, VMEM, HBM, HBM, HBM],
        out_specs=(VMEM, HBM),
        scratch_shapes=[
            pltpu.VMEM((2 * RANK, 24 * RANK), jnp.bfloat16),
            pltpu.VMEM((RANK, RANK, LEAVES), f32),
            pltpu.VMEM((RANK, RANK, 254), f32),
            pltpu.VMEM((4, RANK, RANK, 254), f32),
            pltpu.VMEM((4, 254), jnp.int32),
            pltpu.VMEM((5 * RANK, 8, RANK), f32),
            pltpu.SemaphoreType.DMA((5,)),
        ],
        compiler_params=pltpu.CompilerParams(vmem_limit_bytes=12 * 2**20),
        cost_estimate=pl.CostEstimate(flops=1_000_000_000, bytes_accessed=3_000_000, transcendentals=0),
        name="widen",
    )(
        in_hbm(by_leaf(leaf_spread)),
        weights,
        spread_table,
        coupling_table,
        admissible_table,
    )
    down = pl.pallas_call(
        tree_kernel,
        out_shape=jax.ShapeDtypeStruct((RANK, 128), f32),
        in_specs=[VMEM, HBM, VMEM],
        out_specs=VMEM,
        scratch_shapes=[
            pltpu.VMEM((RANK, VECS, 128), f32),
            pltpu.VMEM((4, RANK, 128), f32),
            pltpu.VMEM((24 * RANK, 256), jnp.bfloat16),
            pltpu.VMEM((2 * RANK, 24 * RANK), jnp.bfloat16),
            pltpu.SemaphoreType.DMA,
        ],
        compiler_params=pltpu.CompilerParams(vmem_limit_bytes=8 * 2**20),
        cost_estimate=pl.CostEstimate(flops=4_000_000_000, bytes_accessed=6_000_000, transcendentals=0),
        name="tree",
    )(gathered, in_hbm(weights), by_leaf(tree_lift))
    out = pl.pallas_call(
        final_kernel,
        out_shape=window,
        in_specs=[VMEM] * 6,
        out_specs=VMEM,
        compiler_params=pltpu.CompilerParams(vmem_limit_bytes=8 * 2**20),
        cost_estimate=pl.CostEstimate(flops=100_000_000, bytes_accessed=3_000_000, transcendentals=0),
        name="final",
    )(down, wide, column_basis, own, chip, far)
    return out.transpose(1, 0, 2).reshape(VECS, LEAVES * 128)


def solution(mesh):
    part = P(AXES, None, None)
    return jax.shard_map(
        local,
        mesh=mesh,
        in_specs=(P(None, AXES), part, P(AXES), P(AXES), P(AXES), part, part, part, part, P(), P(), P(), P()),
        out_specs=P(None, AXES),
        check_vma=False,
    )
```
